256 devices in a mesh: vocab: 64 (over x, y_lo, z), dp: 4 (over y_hi, core).
Axes of the slice: x: 4, y: 4 (y_hi: 2, y_lo: 2; y = y_hi * 2 + y_lo), z: 8, core: 2. Of those that a mesh axis runs over, the one named last changes fastest.
Arguments:
- hidden: bfloat16 [1024, 4096], P('dp', 'vocab'), may hold values from -6 to 6
- head_weight: bfloat16 [77824, 4096], P('vocab'), may hold values from -16 to 16
- teacher_codes: int32 [1024, 77824], P('dp', 'vocab'), may hold values from 1 to 126, as said below
- teacher_scales: int32 [1024, 2432], P('dp', 'vocab'), may hold values from -18 to -9
- loss_cotangent: float32 [1024], P('dp'), may hold values from 0.5 to 5
Outputs:
- hidden_grad: bfloat16 [1024, 4096], P('dp', 'vocab')
- head_grad: bfloat16 [77824, 4096], P('vocab', 'dp')
The draws below stay inside these ranges and needn't reach their ends.
Inputs may be any that keep to these rules, and one draw needn't show every extreme that they name: `teacher_codes`: the sign bit is never set.
All inputs are finite; a program needn't handle non-finite values.
Results may differ from the reference program's by a relative error of at most 0.007.
Values may be sent and summed in bfloat16 or wider, within the bound.
A program may use at most 128 MiB of HBM per device.

```python
import math
import jax
import jax.numpy as jnp
from jax import lax

D = 4096
VOCAB = 77824
TOKENS = 1024


def draw_head_weight(key, part):
    key = jax.random.fold_in(key, 11)
    key_base, key_scale = jax.random.split(key, 2)
    row = jnp.arange(VOCAB).astype(jnp.float32)
    spread = jnp.exp(jax.random.uniform(key_scale, (VOCAB,), jnp.float32) * math.log(10.0))
    scale = spread * (0.75 + 0.5 * row / VOCAB)
    base = jnp.clip(jax.random.normal(key_base, (VOCAB, D), jnp.float32), -6.0, 6.0) / math.sqrt(D)
    weight = scale[:, None] * base
    return weight.astype(jnp.bfloat16)


def draw_teacher_codes(key, part):
    key = jax.random.fold_in(key, 37)
    key_hot, key_high, key_low = jax.random.split(key, 3)
    shape = (TOKENS, VOCAB)
    hot = jax.random.randint(key_hot, shape, 0, 512) == 0
    high = jax.random.randint(key_high, shape, 100, 127)
    low = jax.random.randint(key_low, shape, 1, 49)
    return jnp.where(hot, high, low).astype(jnp.int32)


def draw_teacher_scales(key, part):
    key = jax.random.fold_in(key, 23)
    blocks = VOCAB // 32
    shape = (TOKENS, blocks)
    position = jnp.arange(blocks, dtype=jnp.int32)[None, :]
    shift = 3 * position // blocks
    return (jax.random.randint(key, shape, -16, -8) - shift).astype(jnp.int32)


def block_levels(rng, shape, cuts, smallest, top_value):
    loudness, own = 1.0, jax.random.fold_in(rng, 6)
    for dim, shards_of in cuts:
        draws = jnp.exp(jax.random.uniform(jax.random.fold_in(own, dim), (shards_of,), jnp.float32, smallest / len(cuts), top_value / len(cuts)))
        loudness = loudness * jnp.repeat(draws, shape[dim] // shards_of).reshape([-1 if axis == dim else 1 for axis in range(len(shape))])
    return loudness


def bell_draw(own_key, shape, scale, limit, shards=(), held_as=jnp.bfloat16):
    values = scale * jax.random.normal(own_key, shape, jnp.float32)
    if shards:
        values = values * block_levels(own_key, shape, shards, -0.22, 0.18)
    return jnp.clip(values, -limit, limit).astype(held_as)


def setup_inputs(seed: int = 0) -> dict:
    key_list = jax.random.split(jax.random.key(seed), 6)
    hidden = bell_draw(key_list[0], (TOKENS, D), 1.0, 6.0, ((0, 4), (1, 64)))
    head_weight = draw_head_weight(jax.random.fold_in(key_list[5], 71), 0)
    teacher_codes = draw_teacher_codes(jax.random.fold_in(key_list[5], 71), 0)
    teacher_scales = draw_teacher_scales(jax.random.fold_in(key_list[5], 71), 0)
    loss_cotangent = jnp.clip(jnp.exp(math.log(5.0) - 2.3025851 * jax.random.uniform(key_list[4], (TOKENS,), jnp.float32) ** block_levels(key_list[4], (TOKENS,), ((0, 4),), -0.2, 0.2)), 0.5, 5.0)
    return {"hidden": hidden, "head_weight": head_weight, "teacher_codes": teacher_codes, "teacher_scales": teacher_scales, "loss_cotangent": loss_cotangent}


def decode_teacher(codes, scales):
    field = codes // 8
    mantissa = (codes % 8).astype(jnp.float32)
    normal_value = (8.0 + mantissa) * jnp.exp2((field - 10).astype(jnp.float32))
    tiny_value = mantissa * (2.0 ** -9)
    value = jnp.where(field == 0, tiny_value, normal_value)
    rows, width = codes.shape
    blocks = value.reshape(rows, width // 32, 32) * jnp.exp2(scales.astype(jnp.float32))[:, :, None]
    return blocks.reshape(rows, width)


def reference(hidden, head_weight, teacher_codes, teacher_scales, loss_cotangent):
    logits = lax.dot_general(hidden, head_weight, (((1,), (1,)), ((), ())), preferred_element_type=jnp.float32)
    row_max = jnp.max(logits, axis=1)
    shifted = jnp.exp(logits - row_max[:, None])
    row_sum = jnp.sum(shifted, axis=1)
    probs = shifted / row_sum[:, None]
    teacher = decode_teacher(teacher_codes, teacher_scales)
    teacher_total = jnp.sum(teacher, axis=1)
    token_grad = (loss_cotangent[:, None] * (probs - teacher / teacher_total[:, None])).astype(jnp.bfloat16)
    hidden_grad = jnp.dot(token_grad, head_weight, preferred_element_type=jnp.float32).astype(jnp.bfloat16)
    head_grad = lax.dot_general(token_grad, hidden, (((0,), (0,)), ((), ())), preferred_element_type=jnp.float32)
    return hidden_grad, head_grad.astype(jnp.bfloat16)
```

```python
import jax
import jax.numpy as jnp
from jax import lax
from jax.experimental import pallas as pl
from jax.experimental.pallas import tpu as pltpu
from jax.sharding import PartitionSpec as P

BF = jnp.bfloat16
F32 = jnp.float32
MESH = pl.DeviceIdType.MESH

V = 1216
T = 256
NEAR = (0, 1, 7, 2, 6, 3, 5, 4)
FAR = (4, 3, 5, 2, 6, 1, 7, 0)


def rows(start, size):
    return pl.ds(pl.multiple_of(start, size), size)


def kernel(
    hid,
    scales,
    cot,
    w_hbm,
    codes_hbm,
    hg_out,
    head_out,
    h,
    w,
    codes,
    teach,
    logits,
    tg,
    tg_all,
    hx_all,
    part,
    rx,
    acc,
    qy,
    ry,
    qz,
    rz,
    st,
    st_z,
    st_xy,
    out,
    local_sem,
    out_sem,
    ag_send_z,
    ag_send_y,
    ag_send_x,
    ag_send_x2,
    ag_recv,
    hx_send,
    hx_recv,
    tg_send,
    tg_recv,
    st_send,
    st_recv,
    rs_send,
    rs_recv,
    rp_send,
    rp_recv,
    ry_send,
    ry_recv,
    rz_send,
    rz_recv,
):
    v = lax.axis_index("vocab")
    d = lax.axis_index("dp")
    x, y, z = v // 16, (v // 8) % 2, v % 8
    yh, core = d // 2, d % 2

    def at(dx, dy, dz):
        return ((x + dx) % 4 * 2 + (y + dy) % 2) * 8 + (z + dz) % 8

    def dev(dx, dy, dz):
        return (at(dx, dy, dz), d)

    other = (1 - yh) * 2
    cross = [(at(0, 1, 0), other), (at(0, 1, 0), other + 1)]
    twin = (v, yh * 2 + 1 - core)
    opposite = (v, other + core)

    def remote(src, dst, ss, rs, to):
        return pltpu.make_async_remote_copy(
            src_ref=src, dst_ref=dst, send_sem=ss, recv_sem=rs, device_id=to, device_id_type=MESH
        )

    def arrived(ref, rs):
        remote(ref, ref, local_sem.at[0], rs, twin).wait_recv()

    def sent(ref, ss):
        remote(ref, ref, ss, local_sem.at[0], twin).wait_send()

    barrier = pltpu.get_barrier_semaphore()
    partners = [dev(0, 0, dz) for dz in range(1, 8)]
    partners += [dev(dx, dy, 0) for dx in range(4) for dy in range(2) if dx or dy]
    partners += cross + [twin, opposite]
    for p in partners:
        pl.semaphore_signal(barrier, inc=1, device_id=p, device_id_type=MESH)

    codes_copy = pltpu.make_async_copy(codes_hbm, codes, local_sem.at[1])
    codes_copy.start()
    w_copy = pltpu.make_async_copy(w_hbm, w, local_sem.at[2])
    w_copy.start()

    h[rows(v * 64, 64), :] = hid[...]

    codes_copy.wait()

    def decode(b, total):
        r = rows(b * 32, 32)
        c = codes[r, :]
        field = c >> 3
        mantissa = (c & 7).astype(F32)
        s = scales[pl.ds(b, 1), :]
        digits = jnp.where(field == 0, 2.0 * mantissa, 8.0 + mantissa)
        value = digits * jnp.exp2((field - 10 + s).astype(F32))
        teach[r, :] = value
        return total + value

    total = lax.fori_loop(0, V // 32, decode, jnp.zeros((32, T), F32))
    teacher_sum = jnp.sum(total, axis=0, keepdims=True)

    pl.semaphore_wait(barrier, len(partners))

    def block(dx, dy, k):
        return h.at[rows(at(dx, dy, -NEAR[k]) * 64, 64), :]

    def spread_x(dy, k):
        for i, dx in ((0, 1), (1, -1)):
            b = block(0, dy, k)
            remote(b, b, ag_send_x.at[i, dy, k], ag_recv.at[1 + i, dy, k], dev(dx, 0, 0)).start()

    def spread_y(k):
        b = block(0, 0, k)
        remote(b, b, ag_send_y.at[k], ag_recv.at[0, 1, k], dev(0, 1, 0)).start()

    mine = block(0, 0, 0)
    for k in range(1, 8):
        remote(mine, mine, ag_send_z.at[k], ag_recv.at[0, 0, k], dev(0, 0, NEAR[k])).start()
    for k in range(8):
        if k:
            arrived(block(0, 0, k), ag_recv.at[0, 0, k])
        spread_x(0, k)
        spread_y(k)
    for k in range(8):
        arrived(block(0, 1, k), ag_recv.at[0, 1, k])
        spread_x(1, k)

    def chunk(dx, dy):
        return ((x + dx) % 4 * 2 + (y + dy) % 2) * 512

    def add_logits(start):
        f = rows(start, 512)
        logits[...] += jnp.dot(w[:, f], h[f, :], preferred_element_type=F32)

    logits[...] = jnp.zeros_like(logits)
    w_copy.wait()

    def dots_0(i, _):
        add_logits(chunk(0, i))
        return 0

    lax.fori_loop(0, 2, dots_0, 0)
    for dy in range(2):
        for k in range(8):
            for i, dx in ((0, 1), (1, -1)):
                b = block(-dx, dy, k)
                arrived(b, ag_recv.at[1 + i, dy, k])
                if k % 2 == i:
                    remote(b, b, ag_send_x2.at[dy, k], ag_recv.at[3, dy, k], dev(dx, 0, 0)).start()

    def dots_1(i, _):
        add_logits(chunk(1 + i // 2 * 2, i % 2))
        return 0

    lax.fori_loop(0, 4, dots_1, 0)
    for dy in range(2):
        for k in range(8):
            arrived(block(2, dy, k), ag_recv.at[3, dy, k])

    own_lanes = rows(d * T, T)
    for c2 in range(2):
        src = h.at[rows(((other + c2) * 2 + y) * 512, 512), :]
        dst = hx_all.at[rows(y * 512, 512), own_lanes]
        remote(src, dst, hx_send.at[c2], hx_recv.at[core], cross[c2]).start()
    src = h.at[rows((yh * 2 + 1 - core) * 1024, 1024), :]
    remote(src, hx_all.at[:, own_lanes], hx_send.at[2], hx_recv.at[2], twin).start()
    hx_all[:, own_lanes] = h[rows(d * 1024, 1024), :]

    def dots_2(i, _):
        add_logits(chunk(2, i))
        return 0

    lax.fori_loop(0, 2, dots_2, 0)

    def top(b, m):
        return jnp.maximum(m, logits[rows(b * 32, 32), :])

    m = lax.fori_loop(1, V // 32, top, logits[0:32, :])
    local_max = jnp.max(m, axis=0, keepdims=True)

    def exps(b, s):
        r = rows(b * 32, 32)
        e = jnp.exp(logits[r, :] - local_max)
        logits[r, :] = e
        return s + e

    s = lax.fori_loop(0, V // 32, exps, jnp.zeros((32, T), F32))
    local_sum = jnp.sum(s, axis=0, keepdims=True)

    def share(m, s, t, stage, buf, peers):
        st[stage, 0:1, :] = m
        st[stage, 1:2, :] = s
        st[stage, 2:3, :] = t
        for j, p in enumerate(peers):
            remote(st.at[stage], buf.at[j], st_send.at[stage, j], st_recv.at[stage, j], p).start()
        for j in range(7):
            arrived(buf.at[j], st_recv.at[stage, j])
        best = m
        for j in range(7):
            best = jnp.maximum(best, buf[j, 0:1, :])
        s = s * jnp.exp(m - best)
        for j in range(7):
            s += buf[j, 1:2, :] * jnp.exp(buf[j, 0:1, :] - best)
            t += buf[j, 2:3, :]
        return best, s, t

    st[...] = jnp.zeros_like(st)
    along_z = [dev(0, 0, dz) for dz in FAR[:7]]
    along_xy = [dev(dx, dy, 0) for dx, dy in ((2, 1), (2, 0), (1, 1), (3, 1), (1, 0), (3, 0), (0, 1))]
    row_max, row_sum, row_teach = share(local_max, local_sum, teacher_sum, 0, st_z, along_z)
    row_max, row_sum, row_teach = share(row_max, row_sum, row_teach, 1, st_xy, along_xy)

    up = cot[...] * jnp.exp(local_max - row_max) / row_sum
    down = cot[...] / row_teach

    def grads(b, _):
        r = rows(b * 32, 32)
        g = (logits[r, :] * up - teach[r, :] * down).astype(BF)
        tg[r, :] = g
        tg_all[r, own_lanes] = g
        return 0

    lax.fori_loop(0, V // 32, grads, 0)

    remote(tg, tg_all.at[:, own_lanes], tg_send.at[0], tg_recv.at[0], opposite).start()
    remote(tg, tg_all.at[:, own_lanes], tg_send.at[1], tg_recv.at[1], twin).start()

    def dot_chunk(start):
        return lax.dot_general(
            w[:, rows(start, 512)], tg[...], (((0,), (0,)), ((), ())), preferred_element_type=F32
        )

    def direct(i, _):
        way, slot = i % 2, i // 2
        start = chunk(2 - slot + 2 * slot * way, way + slot)
        f = rows(start, 512)
        part[f, :] = dot_chunk(start).astype(BF)
        to = dev(1 - 2 * way, 0, 0)
        remote(part.at[f, :], rx.at[way, slot], rs_send.at[way, slot], rs_recv.at[way, slot], to).start()
        return 0

    lax.fori_loop(0, 4, direct, 0)

    theirs = pl.ds(pl.multiple_of(other * T, 2 * T), 2 * T)
    for c2 in range(2):
        arrived(hx_all.at[rows((1 - y) * 512, 512), own_lanes], hx_recv.at[c2])
    src = hx_all.at[rows((1 - y) * 512, 512), theirs]
    remote(src, src, hx_send.at[3], hx_recv.at[3], dev(0, 1, 0)).start()

    def combined(way, _):
        start = chunk(1 + 2 * way, way)
        f = rows(start, 512)
        arrived(rx.at[way, 0], rs_recv.at[way, 0])
        part[f, :] = (dot_chunk(start) + rx[way, 0].astype(F32)).astype(BF)
        to = dev(1 - 2 * way, 0, 0)
        for k in range(8):
            zz = (z + FAR[k]) % 8
            src = part.at[rows(start + zz * 64, 64), :]
            dst = rx.at[way, 2, rows(zz * 64, 64), :]
            remote(src, dst, rp_send.at[way, k], rp_recv.at[way, k], to).start()
        return 0

    lax.fori_loop(0, 2, combined, 0)

    def own(dy, _):
        acc[dy] = dot_chunk(chunk(0, dy))
        return 0

    lax.fori_loop(0, 2, own, 0)
    for way in range(2):
        arrived(rx.at[way, 1], rs_recv.at[way, 1])
        acc[1 - way] += rx[way, 1].astype(F32)

    def finish_y(k):
        zz = (z + FAR[k]) % 8
        r = rows(zz * 64, 64)
        for way in (1, 0):
            arrived(rx.at[way, 2, r, :], rp_recv.at[way, k])
            total = acc[way, r, :] + rx[way, 2, r, :].astype(F32)
            if way:
                qy[r, :] = total.astype(BF)
                src = qy.at[r, :]
                remote(src, ry.at[r, :], ry_send.at[k], ry_recv.at[k], dev(0, 1, 0)).start()
            else:
                acc[0, r, :] = total

    def finish_z(k):
        zz = (z + FAR[k]) % 8
        r = rows(zz * 64, 64)
        arrived(ry.at[r, :], ry_recv.at[k])
        total = acc[0, r, :] + ry[r, :].astype(F32)
        if k == 7:
            return total
        qz[r, :] = total.astype(BF)
        remote(qz.at[r, :], rz.at[k], rz_send.at[k], rz_recv.at[k], dev(0, 0, FAR[k])).start()

    mine = None
    for k in range(9):
        if k < 8:
            finish_y(k)
        if k > 0:
            mine = finish_z(k - 1)
    acc[0, 0:64, :] = mine

    arrived(tg_all.at[:, own_lanes], tg_recv.at[0])
    src = tg_all.at[:, rows((other + core) * T, T)]
    remote(src, src, tg_send.at[2], tg_recv.at[2], twin).start()
    arrived(tg_all.at[:, own_lanes], tg_recv.at[1])
    arrived(hx_all.at[:, own_lanes], hx_recv.at[2])
    arrived(hx_all.at[rows(y * 512, 512), theirs], hx_recv.at[3])
    arrived(tg_all.at[:, own_lanes], tg_recv.at[2])

    def head(i, _):
        r = rows(i * 304, 304)
        out[r, :] = lax.dot_general(
            tg_all[r, :], hx_all[...], (((1,), (1,)), ((), ())), preferred_element_type=F32
        ).astype(BF)
        pltpu.make_async_copy(out.at[r, :], head_out.at[r, :], out_sem.at[i]).start()
        return 0

    lax.fori_loop(0, 4, head, 0)

    total = acc[0, 0:64, :]
    for k in range(7):
        arrived(rz.at[k], rz_recv.at[k])
        total += rz[k].astype(F32)
    hg_out[...] = total.astype(BF)

    for i in range(4):
        r = rows(i * 304, 304)
        pltpu.make_async_copy(out.at[r, :], head_out.at[r, :], out_sem.at[i]).wait()
    one = h.at[0:64, :]
    for k in range(8):
        if k:
            sent(one, ag_send_z.at[k])
        sent(one, ag_send_y.at[k])
        for dy in range(2):
            sent(one, ag_send_x.at[0, dy, k])
            sent(one, ag_send_x.at[1, dy, k])
            sent(one, ag_send_x2.at[dy, k])
    for c2 in range(2):
        sent(h.at[0:512, :], hx_send.at[c2])
    sent(h.at[0:1024, :], hx_send.at[2])
    sent(hx_all.at[rows((1 - y) * 512, 512), theirs], hx_send.at[3])
    for i in range(3):
        sent(tg, tg_send.at[i])
    for i in range(2):
        for j in range(7):
            sent(st.at[i], st_send.at[i, j])
        sent(rx.at[i, 0], rs_send.at[i, 0])
        sent(rx.at[i, 1], rs_send.at[i, 1])
        for k in range(8):
            sent(one, rp_send.at[i, k])
    for k in range(8):
        sent(one, ry_send.at[k])
        if k < 7:
            sent(one, rz_send.at[k])


def per_device(hidden, head_weight, teacher_codes, teacher_scales, loss_cotangent):
    dma = pltpu.SemaphoreType.DMA
    vmem = pl.BlockSpec(memory_space=pltpu.VMEM)
    hbm = pl.BlockSpec(memory_space=pl.ANY)
    hidden_grad, head_grad = pl.pallas_call(
        kernel,
        name="head_backward",
        out_shape=(
            jax.ShapeDtypeStruct((64, T), BF),
            jax.ShapeDtypeStruct((V, 1024), BF),
        ),
        in_specs=[vmem, vmem, vmem, hbm, hbm],
        out_specs=(vmem, hbm),
        scratch_shapes=[
            pltpu.VMEM((4096, T), BF),
            pltpu.VMEM((V, 4096), BF),
            pltpu.VMEM((V, T), jnp.int32),
            pltpu.VMEM((V, T), F32),
            pltpu.VMEM((V, T), F32),
            pltpu.VMEM((V, T), BF),
            pltpu.VMEM((V, 4 * T), BF),
            pltpu.VMEM((1024, 4 * T), BF),
            pltpu.VMEM((4096, T), BF),
            pltpu.VMEM((2, 3, 512, T), BF),
            pltpu.VMEM((2, 512, T), F32),
            pltpu.VMEM((512, T), BF),
            pltpu.VMEM((512, T), BF),
            pltpu.VMEM((512, T), BF),
            pltpu.VMEM((7, 64, T), BF),
            pltpu.VMEM((2, 8, T), F32),
            pltpu.VMEM((7, 8, T), F32),
            pltpu.VMEM((7, 8, T), F32),
            pltpu.VMEM((V, 1024), BF),
            dma((3,)),
            dma((4,)),
            dma((8,)),
            dma((8,)),
            dma((2, 2, 8)),
            dma((2, 8)),
            dma((4, 2, 8)),
            dma((4,)),
            dma((4,)),
            dma((3,)),
            dma((3,)),
            dma((2, 7)),
            dma((2, 7)),
            dma((2, 2)),
            dma((2, 2)),
            dma((2, 8)),
            dma((2, 8)),
            dma((8,)),
            dma((8,)),
            dma((8,)),
            dma((8,)),
        ],
        compiler_params=pltpu.CompilerParams(
            collective_id=0, has_side_effects=True, vmem_limit_bytes=56 << 20
        ),
        cost_estimate=pl.CostEstimate(
            flops=6 * V * T * 4096, bytes_accessed=14 << 20, transcendentals=2 * V * T
        ),
    )(hidden.T, teacher_scales.T, loss_cotangent.reshape(1, T), head_weight, teacher_codes.T)
    return hidden_grad.T, head_grad


def solution(mesh):
    return jax.shard_map(
        per_device,
        mesh=mesh,
        in_specs=(P("dp", "vocab"), P("vocab", None), P("dp", "vocab"), P("dp", "vocab"), P("dp")),
        out_specs=(P("dp", "vocab"), P("vocab", "dp")),
        check_vma=False,
    )
```

```python
import jax
import jax.numpy as jnp
from jax import lax
from jax.experimental import pallas as pl
from jax.experimental.pallas import tpu as pltpu
from jax.sharding import PartitionSpec as P

BF = jnp.bfloat16
F32 = jnp.float32
MESH = pl.DeviceIdType.MESH

V = 1216
T = 256
NEAR = (0, 1, 7, 2, 6, 3, 5, 4)
FAR = (4, 3, 5, 2, 6, 1, 7, 0)


def rows(start, size):
    return pl.ds(pl.multiple_of(start, size), size)


def kernel(
    hid_hbm,
    scales_hbm,
    cot_hbm,
    w_hbm,
    codes_hbm,
    hg_out,
    head_out,
    scales,
    cot,
    h,
    w,
    codes,
    teach,
    logits,
    tg,
    tg_all,
    hx_all,
    part,
    rx,
    rf,
    qf,
    ro,
    acc,
    qy,
    ry,
    qz,
    rz,
    st,
    st_z,
    st_xy,
    local_sem,
    ag_send_z,
    ag_send_y,
    ag_send_x,
    ag_recv,
    hx_send,
    hx_recv,
    tg_send,
    tg_recv,
    st_send,
    st_recv,
    rs_send,
    rs_recv,
    rf_send,
    rf_recv,
    ro_send,
    ro_recv,
    ry_send,
    ry_recv,
    rz_send,
    rz_recv,
):
    v = lax.axis_index("vocab")
    d = lax.axis_index("dp")
    x, y, z = v // 16, (v // 8) % 2, v % 8
    yh, core = d // 2, d % 2

    def at(dx, dy, dz):
        return ((x + dx) % 4 * 2 + (y + dy) % 2) * 8 + (z + dz) % 8

    def dev(dx, dy, dz):
        return (at(dx, dy, dz), d)

    other = (1 - yh) * 2
    cross = [(at(0, 1, 0), other), (at(0, 1, 0), other + 1)]
    twin = (v, yh * 2 + 1 - core)
    opposite = (v, other + core)

    def remote(src, dst, ss, rs, to):
        return pltpu.make_async_remote_copy(
            src_ref=src, dst_ref=dst, send_sem=ss, recv_sem=rs, device_id=to, device_id_type=MESH
        )

    def arrived(ref, rs):
        remote(ref, ref, local_sem.at[0], rs, twin).wait_recv()

    def sent(ref, ss):
        remote(ref, ref, ss, local_sem.at[0], twin).wait_send()

    barrier = pltpu.get_barrier_semaphore()
    partners = [dev(0, 0, dz) for dz in range(1, 8)]
    partners += [dev(dx, dy, 0) for dx in range(4) for dy in range(2) if dx or dy]
    partners += cross + [twin, opposite]
    for p in partners:
        pl.semaphore_signal(barrier, inc=1, device_id=p, device_id_type=MESH)

    loads = [
        pltpu.make_async_copy(src, dst, local_sem.at[1 + i])
        for i, (src, dst) in enumerate(
            (
                (hid_hbm, h.at[rows(v * 64, 64), :]),
                (scales_hbm, scales),
                (codes_hbm, codes),
                (cot_hbm, cot),
                (w_hbm, w),
            )
        )
    ]
    for load in loads:
        load.start()

    loads[1].wait()
    loads[2].wait()

    def decode(b, total):
        r = rows(b * 32, 32)
        c = codes[r, :]
        field = c >> 3
        mantissa = (c & 7).astype(F32)
        s = scales[pl.ds(b, 1), :]
        digits = jnp.where(field == 0, 2.0 * mantissa, 8.0 + mantissa)
        value = digits * jnp.exp2((field - 10 + s).astype(F32))
        teach[r, :] = value
        return total + value

    total = lax.fori_loop(0, V // 32, decode, jnp.zeros((32, T), F32))
    teacher_sum = jnp.sum(total, axis=0, keepdims=True)

    loads[0].wait()
    loads[3].wait()
    pl.semaphore_wait(barrier, len(partners))

    def block(dx, dy, k):
        return h.at[rows(at(dx, dy, -NEAR[k]) * 64, 64), :]

    def pass_on(b, ss, rs, to):
        remote(b, b, ss, rs, to).start()

    def spread_x(dy, k):
        for i, dx in ((0, 1), (1, -1)):
            pass_on(block(0, dy, k), ag_send_x.at[i, dy, k], ag_recv.at[2 + i, dy, k], dev(dx, 0, 0))

    def spread_y(far, k):
        pass_on(block(2 * far, 0, k), ag_send_y.at[far, k], ag_recv.at[far, 1, k], dev(0, 1, 0))

    def spread_z(far):
        for k in range(1, 8):
            pass_on(block(2 * far, 0, 0), ag_send_z.at[far, k], ag_recv.at[far, 0, k], dev(0, 0, NEAR[k]))

    def chunk(dx, dy):
        return ((x + dx) % 4 * 2 + (y + dy) % 2) * 512

    own_lanes = rows(d * T, T)

    def hidden_across(dx):
        quarter = (x + dx) % 4

        @pl.when(quarter // 2 == 1 - yh)
        def _():
            c2 = quarter % 2
            src = h.at[rows(chunk(dx, 0), 512), :]
            dst = hx_all.at[rows(y * 512, 512), own_lanes]
            to = (at(0, 1, 0), other + c2)
            remote(src, dst, hx_send.at[c2], hx_recv.at[core], to).start()

    pass_on(block(0, 0, 0), ag_send_z.at[0, 0], ag_recv.at[1, 0, 0], dev(2, 0, 0))
    spread_z(0)
    spread_x(0, 0)
    spread_y(0, 0)
    for k in range(1, 8):
        arrived(block(0, 0, k), ag_recv.at[0, 0, k])
        spread_x(0, k)
        spread_y(0, k)
        if k == 2:
            arrived(block(2, 0, 0), ag_recv.at[1, 0, 0])
            spread_z(1)
            spread_y(1, 0)
    hidden_across(0)
    for k in range(8):
        arrived(block(0, 1, k), ag_recv.at[0, 1, k])
        spread_x(1, k)
        if k:
            arrived(block(2, 0, k), ag_recv.at[1, 0, k])
            spread_y(1, k)
    hidden_across(2)

    def add_logits(start):
        f = rows(start, 512)
        logits[...] += jnp.dot(w[:, f], h[f, :], preferred_element_type=F32)

    logits[...] = jnp.zeros_like(logits)
    loads[4].wait()

    def dots_near(i, _):
        add_logits(chunk(0, i))
        return 0

    lax.fori_loop(0, 2, dots_near, 0)
    add_logits(chunk(2, 0))
    for dy in range(2):
        for k in range(8):
            for i, dx in ((0, 1), (1, -1)):
                arrived(block(-dx, dy, k), ag_recv.at[2 + i, dy, k])
        if dy == 0:
            hidden_across(1)
            hidden_across(3)

            def dots_side(i, _):
                add_logits(chunk(1 + 2 * i, 0))
                return 0

            lax.fori_loop(0, 2, dots_side, 0)
    for k in range(8):
        arrived(block(2, 1, k), ag_recv.at[1, 1, k])
    src = h.at[rows((yh * 2 + 1 - core) * 1024, 1024), :]
    remote(src, hx_all.at[:, own_lanes], hx_send.at[2], hx_recv.at[2], twin).start()
    hx_all[:, own_lanes] = h[rows(d * 1024, 1024), :]

    def dots_last(i, _):
        add_logits(chunk(1 + i, 1))
        return 0

    lax.fori_loop(0, 3, dots_last, 0)

    def top(b, m):
        return jnp.maximum(m, logits[rows(b * 32, 32), :])

    m = lax.fori_loop(1, V // 32, top, logits[0:32, :])
    local_max = jnp.max(m, axis=0, keepdims=True)

    def exps(b, s):
        r = rows(b * 32, 32)
        e = jnp.exp(logits[r, :] - local_max)
        logits[r, :] = e
        return s + e

    s = lax.fori_loop(0, V // 32, exps, jnp.zeros((32, T), F32))
    local_sum = jnp.sum(s, axis=0, keepdims=True)

    def hidden_along():
        for c2 in range(2):
            lanes = rows((other + c2) * T, T)
            src = hx_all.at[rows((1 - y) * 512, 512), lanes]
            arrived(src, hx_recv.at[c2])
            remote(src, src, hx_send.at[3 + c2], hx_recv.at[3 + c2], dev(0, 1, 0)).start()

    def share(m, s, t, stage, buf, peers):
        st[stage, 0:1, :] = m
        st[stage, 1:2, :] = s
        st[stage, 2:3, :] = t
        for j, p in enumerate(peers):
            remote(st.at[stage], buf.at[j], st_send.at[stage, j], st_recv.at[stage, j], p).start()
        if stage:
            hidden_along()
        for j in range(7):
            arrived(buf.at[j], st_recv.at[stage, j])
        best = m
        for j in range(7):
            best = jnp.maximum(best, buf[j, 0:1, :])
        s = s * jnp.exp(m - best)
        for j in range(7):
            s += buf[j, 1:2, :] * jnp.exp(buf[j, 0:1, :] - best)
            t += buf[j, 2:3, :]
        return best, s, t

    st[...] = jnp.zeros_like(st)
    along_z = [dev(0, 0, dz) for dz in FAR[:7]]
    along_xy = [dev(dx, dy, 0) for dx, dy in ((2, 1), (2, 0), (1, 1), (3, 1), (1, 0), (3, 0), (0, 1))]
    row_max, row_sum, row_teach = share(local_max, local_sum, teacher_sum, 0, st_z, along_z)
    row_max, row_sum, row_teach = share(row_max, row_sum, row_teach, 1, st_xy, along_xy)

    up = cot[...] * jnp.exp(local_max - row_max) / row_sum
    down = cot[...] / row_teach

    def grads(b, _):
        r = rows(b * 32, 32)
        g = (logits[r, :] * up - teach[r, :] * down).astype(BF)
        tg[r, :] = g
        tg_all[r, own_lanes] = g
        return 0

    lax.fori_loop(0, V // 32, grads, 0)

    remote(tg, tg_all.at[:, own_lanes], tg_send.at[0], tg_recv.at[0], opposite).start()
    remote(tg, tg_all.at[:, own_lanes], tg_send.at[1], tg_recv.at[1], twin).start()

    def dot_chunk(start):
        return lax.dot_general(
            w[:, rows(start, 512)], tg[...], (((0,), (0,)), ((), ())), preferred_element_type=F32
        )

    def far(dy, _):
        start = chunk(2, dy)
        part[rows(start, 512), :] = dot_chunk(start).astype(BF)
        for k in range(7):
            src = part.at[rows(start + (z + FAR[k]) % 8 * 64, 64), :]
            remote(src, rf.at[dy, k], rf_send.at[dy, k], rf_recv.at[dy, k], dev(0, 0, FAR[k])).start()
        return 0

    lax.fori_loop(0, 2, far, 0)

    def side(i, _):
        way, dy = i % 2, 1 - i // 2
        start = chunk(1 + 2 * way, dy)
        part[rows(start, 512), :] = dot_chunk(start).astype(BF)
        for k in range(8):
            zz = (z + FAR[k]) % 8
            src = part.at[rows(start + zz * 64, 64), :]
            dst = rx.at[way, dy, rows(zz * 64, 64), :]
            remote(src, dst, rs_send.at[way, dy, k], rs_recv.at[way, dy, k], dev(1 - 2 * way, 0, 0)).start()
        return 0

    lax.fori_loop(0, 4, side, 0)

    def own(dy, _):
        acc[dy] = dot_chunk(chunk(0, dy))
        return 0

    lax.fori_loop(0, 2, own, 0)

    def with_sides(dy, k, r):
        total = acc[dy, r, :]
        for way in range(2):
            arrived(rx.at[way, dy, r, :], rs_recv.at[way, dy, k])
            total += rx[way, dy, r, :].astype(F32)
        return total

    for k in range(8):
        r = rows((z + FAR[k]) % 8 * 64, 64)
        qy[r, :] = with_sides(1, k, r).astype(BF)
        remote(qy.at[r, :], ry.at[r, :], ry_send.at[k], ry_recv.at[k], dev(0, 1, 0)).start()
    for k in range(8):
        r = rows((z + FAR[k]) % 8 * 64, 64)
        total = with_sides(0, k, r)
        arrived(ry.at[r, :], ry_recv.at[k])
        total += ry[r, :].astype(F32)
        if k < 7:
            qz[r, :] = total.astype(BF)
            remote(qz.at[r, :], rz.at[k], rz_send.at[k], rz_recv.at[k], dev(0, 0, FAR[k])).start()
        else:
            acc[0, 0:64, :] = total

    for dy in range(2):
        total = part[rows(chunk(2, dy) + z * 64, 64), :].astype(F32)
        for k in range(7):
            arrived(rf.at[dy, k], rf_recv.at[dy, k])
            total += rf[dy, k].astype(F32)
        qf[dy] = total.astype(BF)
        remote(qf.at[dy], ro.at[dy], ro_send.at[dy], ro_recv.at[dy], dev(2, dy, 0)).start()

    arrived(tg_all.at[:, own_lanes], tg_recv.at[0])
    src = tg_all.at[:, rows((other + core) * T, T)]
    remote(src, src, tg_send.at[2], tg_recv.at[2], twin).start()
    arrived(tg_all.at[:, own_lanes], tg_recv.at[1])
    arrived(hx_all.at[:, own_lanes], hx_recv.at[2])
    for c2 in range(2):
        arrived(hx_all.at[rows(y * 512, 512), own_lanes], hx_recv.at[3 + c2])
    arrived(tg_all.at[:, own_lanes], tg_recv.at[2])

    def head(i, _):
        r = rows(i * 304, 304)
        head_out[r, :] = lax.dot_general(
            tg_all[r, :], hx_all[...], (((1,), (1,)), ((), ())), preferred_element_type=F32
        ).astype(BF)
        return 0

    lax.fori_loop(0, 4, head, 0)

    total = acc[0, 0:64, :]
    for k in range(7):
        arrived(rz.at[k], rz_recv.at[k])
        total += rz[k].astype(F32)
    for dy in range(2):
        arrived(ro.at[dy], ro_recv.at[dy])
        total += ro[dy].astype(F32)
    hg_out[...] = total.astype(BF)

    one = h.at[0:64, :]
    for k in range(8):
        for f in range(2):
            if k or not f:
                sent(one, ag_send_z.at[f, k])
            sent(one, ag_send_y.at[f, k])
            sent(one, ag_send_x.at[0, f, k])
            sent(one, ag_send_x.at[1, f, k])
            sent(one, rs_send.at[0, f, k])
            sent(one, rs_send.at[1, f, k])
            if k < 7:
                sent(one, rf_send.at[f, k])
        sent(one, ry_send.at[k])
        if k < 7:
            sent(one, rz_send.at[k])
    for i in range(2):
        sent(h.at[0:512, :], hx_send.at[i])
        sent(h.at[0:512, :], hx_send.at[3 + i])
        sent(one, ro_send.at[i])
        for j in range(7):
            sent(st.at[i], st_send.at[i, j])
    sent(h.at[0:1024, :], hx_send.at[2])
    for i in range(3):
        sent(tg, tg_send.at[i])


def per_device(hidden, head_weight, teacher_codes, teacher_scales, loss_cotangent):
    dma = pltpu.SemaphoreType.DMA
    vmem = pl.BlockSpec(memory_space=pltpu.VMEM)
    hbm = pl.BlockSpec(memory_space=pltpu.HBM)
    hidden_grad, head_grad = pl.pallas_call(
        kernel,
        name="head_backward",
        out_shape=(
            jax.ShapeDtypeStruct((64, T), BF),
            jax.ShapeDtypeStruct((V, 1024), BF),
        ),
        in_specs=[hbm] * 5,
        out_specs=(vmem, vmem),
        scratch_shapes=[
            pltpu.VMEM((38, T), jnp.int32),
            pltpu.VMEM((1, T), F32),
            pltpu.VMEM((4096, T), BF),
            pltpu.VMEM((V, 4096), BF),
            pltpu.VMEM((V, T), jnp.int32),
            pltpu.VMEM((V, T), F32),
            pltpu.VMEM((V, T), F32),
            pltpu.VMEM((V, T), BF),
            pltpu.VMEM((V, 4 * T), BF),
            pltpu.VMEM((1024, 4 * T), BF),
            pltpu.VMEM((4096, T), BF),
            pltpu.VMEM((2, 2, 512, T), BF),
            pltpu.VMEM((2, 7, 64, T), BF),
            pltpu.VMEM((2, 64, T), BF),
            pltpu.VMEM((2, 64, T), BF),
            pltpu.VMEM((2, 512, T), F32),
            pltpu.VMEM((512, T), BF),
            pltpu.VMEM((512, T), BF),
            pltpu.VMEM((512, T), BF),
            pltpu.VMEM((7, 64, T), BF),
            pltpu.VMEM((2, 8, T), F32),
            pltpu.VMEM((7, 8, T), F32),
            pltpu.VMEM((7, 8, T), F32),
            dma((6,)),
            dma((2, 8)),
            dma((2, 8)),
            dma((2, 2, 8)),
            dma((4, 2, 8)),
            dma((5,)),
            dma((5,)),
            dma((3,)),
            dma((3,)),
            dma((2, 7)),
            dma((2, 7)),
            dma((2, 2, 8)),
            dma((2, 2, 8)),
            dma((2, 7)),
            dma((2, 7)),
            dma((2,)),
            dma((2,)),
            dma((8,)),
            dma((8,)),
            dma((7,)),
            dma((7,)),
        ],
        compiler_params=pltpu.CompilerParams(
            collective_id=0, has_side_effects=True, vmem_limit_bytes=48 << 20
        ),
        cost_estimate=pl.CostEstimate(
            flops=6 * V * T * 4096, bytes_accessed=14 << 20, transcendentals=2 * V * T
        ),
    )(*(
        pltpu.with_memory_space_constraint(a, pltpu.HBM)
        for a in (hidden.T, teacher_scales.T, loss_cotangent.reshape(1, T), head_weight, teacher_codes.T)
    ))
    return hidden_grad.T, head_grad


def solution(mesh):
    return jax.shard_map(
        per_device,
        mesh=mesh,
        in_specs=(P("dp", "vocab"), P("vocab", None), P("dp", "vocab"), P("dp", "vocab"), P("dp")),
        out_specs=(P("dp", "vocab"), P("vocab", "dp")),
        check_vma=False,
    )
```

```python
import jax
import jax.numpy as jnp
from jax import lax
from jax.experimental import pallas as pl
from jax.experimental.pallas import tpu as pltpu
from jax.sharding import PartitionSpec as P

BF = jnp.bfloat16
F32 = jnp.float32
MESH = pl.DeviceIdType.MESH

V = 1216
T = 256
EARLY = 4
NEAR = (0, 1, 7, 2, 6, 3, 5, 4)
FAR = (4, 3, 5, 2, 6, 1, 7, 0)


def rows(start, size):
    return pl.ds(pl.multiple_of(start, size), size)


def kernel(
    hid_hbm,
    scales_hbm,
    cot_hbm,
    w_hbm,
    codes_hbm,
    hg_out,
    head_out,
    scales,
    cot,
    h,
    w,
    codes,
    teach,
    logits,
    tg,
    tg_all,
    hx_all,
    part,
    rx,
    rf,
    qf,
    ro,
    acc,
    qy,
    ry,
    qz,
    rz,
    st,
    st_z,
    st_xy,
    local_sem,
    ag_send_z,
    ag_send_y,
    ag_send_x,
    ag_recv,
    hx_send,
    hx_recv,
    tg_send,
    tg_recv,
    st_send,
    st_recv,
    rs_send,
    rs_recv,
    rf_send,
    rf_recv,
    ro_send,
    ro_recv,
    ry_send,
    ry_recv,
    rz_send,
    rz_recv,
):
    v = lax.axis_index("vocab")
    d = lax.axis_index("dp")
    x, y, z = v // 16, (v // 8) % 2, v % 8
    yh, core = d // 2, d % 2

    def at(dx, dy, dz):
        return ((x + dx) % 4 * 2 + (y + dy) % 2) * 8 + (z + dz) % 8

    def dev(dx, dy, dz):
        return (at(dx, dy, dz), d)

    other = (1 - yh) * 2
    cross = [(at(0, 1, 0), other), (at(0, 1, 0), other + 1)]
    twin = (v, yh * 2 + 1 - core)
    opposite = (v, other + core)

    def remote(src, dst, ss, rs, to):
        return pltpu.make_async_remote_copy(
            src_ref=src, dst_ref=dst, send_sem=ss, recv_sem=rs, device_id=to, device_id_type=MESH
        )

    def arrived(ref, rs):
        remote(ref, ref, local_sem.at[0], rs, twin).wait_recv()

    def sent(ref, ss):
        remote(ref, ref, ss, local_sem.at[0], twin).wait_send()

    barrier = pltpu.get_barrier_semaphore()
    partners = [dev(0, 0, dz) for dz in range(1, 8)]
    partners += [dev(dx, dy, 0) for dx in range(4) for dy in range(2) if dx or dy]
    partners += cross + [twin, opposite]
    for p in partners:
        pl.semaphore_signal(barrier, inc=1, device_id=p, device_id_type=MESH)

    loads = [
        pltpu.make_async_copy(src, dst, local_sem.at[1 + i])
        for i, (src, dst) in enumerate(
            (
                (hid_hbm, h.at[rows(v * 64, 64), :]),
                (scales_hbm, scales),
                (codes_hbm, codes),
                (cot_hbm, cot),
                (w_hbm, w),
            )
        )
    ]
    for load in loads:
        load.start()

    loads[1].wait()
    loads[2].wait()

    def decode(b, total):
        r = rows(b * 32, 32)
        c = codes[r, :]
        field = c >> 3
        mantissa = (c & 7).astype(F32)
        s = scales[pl.ds(b, 1), :]
        digits = jnp.where(field == 0, 2.0 * mantissa, 8.0 + mantissa)
        value = digits * jnp.exp2((field - 10 + s).astype(F32))
        teach[r, :] = value
        return total + value

    total = lax.fori_loop(0, V // 32, decode, jnp.zeros((32, T), F32))
    teacher_sum = jnp.sum(total, axis=0, keepdims=True)

    loads[0].wait()
    loads[3].wait()
    pl.semaphore_wait(barrier, len(partners))

    def block(dx, dy, k):
        return h.at[rows(at(dx, dy, -NEAR[k]) * 64, 64), :]

    def pass_on(b, ss, rs, to):
        remote(b, b, ss, rs, to).start()

    def spread_x(dy, k):
        for i, dx in ((0, 1), (1, -1)):
            pass_on(block(0, dy, k), ag_send_x.at[i, dy, k], ag_recv.at[2 + i, dy, k], dev(dx, 0, 0))

    def spread_y(far, k):
        pass_on(block(2 * far, 0, k), ag_send_y.at[far, k], ag_recv.at[far, 1, k], dev(0, 1, 0))

    def spread_z(far):
        for k in range(1, 8):
            pass_on(block(2 * far, 0, 0), ag_send_z.at[far, k], ag_recv.at[far, 0, k], dev(0, 0, NEAR[k]))

    def chunk(dx, dy):
        return ((x + dx) % 4 * 2 + (y + dy) % 2) * 512

    own_lanes = rows(d * T, T)

    def hidden_across(dx, dy):
        quarter = (x + dx) % 4

        @pl.when(quarter // 2 == 1 - yh)
        def _():
            c2 = quarter % 2
            src = h.at[rows(chunk(dx, dy), 512), :]
            dst = hx_all.at[rows((y + dy) % 2 * 512, 512), own_lanes]
            to = (at(0, 1, 0), other + c2)
            remote(src, dst, hx_send.at[c2, dy], hx_recv.at[core, dy], to).start()

    pass_on(block(0, 0, 0), ag_send_z.at[0, 0], ag_recv.at[1, 0, 0], dev(2, 0, 0))
    spread_z(0)
    spread_x(0, 0)
    spread_y(0, 0)
    for k in range(1, 8):
        arrived(block(0, 0, k), ag_recv.at[0, 0, k])
        spread_x(0, k)
        spread_y(0, k)
        if k == 2:
            arrived(block(2, 0, 0), ag_recv.at[1, 0, 0])
            spread_z(1)
            spread_y(1, 0)
    hidden_across(0, 0)
    for k in range(8):
        arrived(block(0, 1, k), ag_recv.at[0, 1, k])
        spread_x(1, k)
        if k:
            arrived(block(2, 0, k), ag_recv.at[1, 0, k])
            spread_y(1, k)
    hidden_across(0, 1)
    hidden_across(2, 0)

    def add_logits(start):
        f = rows(start, 512)
        logits[...] += jnp.dot(w[:, f], h[f, :], preferred_element_type=F32)

    logits[...] = jnp.zeros_like(logits)
    loads[4].wait()

    def dots_near(i, _):
        add_logits(chunk(0, i))
        return 0

    lax.fori_loop(0, 2, dots_near, 0)
    add_logits(chunk(2, 0))
    for dy in range(2):
        for k in range(8):
            for i, dx in ((0, 1), (1, -1)):
                arrived(block(-dx, dy, k), ag_recv.at[2 + i, dy, k])
        hidden_across(1, dy)
        hidden_across(3, dy)
        if dy == 0:

            def dots_side(i, _):
                add_logits(chunk(1 + 2 * i, 0))
                return 0

            lax.fori_loop(0, 2, dots_side, 0)
    for k in range(8):
        arrived(block(2, 1, k), ag_recv.at[1, 1, k])
    hidden_across(2, 1)
    src = h.at[rows((yh * 2 + 1 - core) * 1024, 1024), :]
    remote(src, hx_all.at[:, own_lanes], hx_send.at[2, 0], hx_recv.at[2, 0], twin).start()
    hx_all[:, own_lanes] = h[rows(d * 1024, 1024), :]

    def dots_last(i, _):
        add_logits(chunk(1 + i, 1))
        return 0

    lax.fori_loop(0, 3, dots_last, 0)

    def top(b, m):
        return jnp.maximum(m, logits[rows(b * 32, 32), :])

    m = lax.fori_loop(1, V // 32, top, logits[0:32, :])
    local_max = jnp.max(m, axis=0, keepdims=True)

    def exps(b, s):
        r = rows(b * 32, 32)
        e = jnp.exp(logits[r, :] - local_max)
        logits[r, :] = e
        return s + e

    s = lax.fori_loop(0, V // 32, exps, jnp.zeros((32, T), F32))
    local_sum = jnp.sum(s, axis=0, keepdims=True)

    def share(m, s, t, stage, buf, peers):
        for n, value in enumerate((m, s, t)):
            for half in range(2):
                st[stage, 2 * n + half : 2 * n + half + 1, :] = value[:, half * 128 : half * 128 + 128]
        for j, p in enumerate(peers):
            remote(st.at[stage], buf.at[j], st_send.at[stage, j], st_recv.at[stage, j], p).start()
        for j in range(7):
            arrived(buf.at[j], st_recv.at[stage, j])
        m, s, t = (st[stage, 2 * n : 2 * n + 2, :] for n in range(3))
        best = m
        for j in range(7):
            best = jnp.maximum(best, buf[j, 0:2, :])
        s = s * jnp.exp(m - best)
        for j in range(7):
            s += buf[j, 2:4, :] * jnp.exp(buf[j, 0:2, :] - best)
            t += buf[j, 4:6, :]
        return tuple(jnp.concatenate([a[0:1, :], a[1:2, :]], axis=1) for a in (best, s, t))

    st[...] = jnp.zeros_like(st)
    along_z = [dev(0, 0, dz) for dz in FAR[:7]]
    along_xy = [dev(dx, dy, 0) for dx, dy in ((2, 1), (2, 0), (1, 1), (3, 1), (1, 0), (3, 0), (0, 1))]
    row_max, row_sum, row_teach = share(local_max, local_sum, teacher_sum, 0, st_z, along_z)
    row_max, row_sum, row_teach = share(row_max, row_sum, row_teach, 1, st_xy, along_xy)

    up = cot[...] * jnp.exp(local_max - row_max) / row_sum
    down = cot[...] / row_teach

    def grads(b, _):
        r = rows(b * 32, 32)
        g = (logits[r, :] * up - teach[r, :] * down).astype(BF)
        tg[r, :] = g
        tg_all[r, own_lanes] = g
        return 0

    lax.fori_loop(0, V // 32, grads, 0)

    def tile(i):
        return rows(i * 304, 304)

    def tokens_across(i):
        dst = tg_all.at[tile(i), own_lanes]
        remote(tg.at[tile(i), :], dst, tg_send.at[i], tg_recv.at[i], opposite).start()

    for i in range(EARLY):
        tokens_across(i)
    remote(tg, tg_all.at[:, own_lanes], tg_send.at[8], tg_recv.at[8], twin).start()

    def dot_chunk(start):
        return lax.dot_general(
            w[:, rows(start, 512)], tg[...], (((0,), (0,)), ((), ())), preferred_element_type=F32
        )

    def far(dy, _):
        start = chunk(2, dy)
        part[rows(start, 512), :] = dot_chunk(start).astype(BF)
        for k in range(7):
            src = part.at[rows(start + (z + FAR[k]) % 8 * 64, 64), :]
            remote(src, rf.at[dy, k], rf_send.at[dy, k], rf_recv.at[dy, k], dev(0, 0, FAR[k])).start()
        return 0

    lax.fori_loop(0, 2, far, 0)

    def side(i, _):
        way, dy = i % 2, 1 - i // 2
        start = chunk(1 + 2 * way, dy)
        part[rows(start, 512), :] = dot_chunk(start).astype(BF)
        for k in range(8):
            zz = (z + FAR[k]) % 8
            src = part.at[rows(start + zz * 64, 64), :]
            dst = rx.at[way, dy, rows(zz * 64, 64), :]
            remote(src, dst, rs_send.at[way, dy, k], rs_recv.at[way, dy, k], dev(1 - 2 * way, 0, 0)).start()
        return 0

    lax.fori_loop(0, 4, side, 0)

    def own(dy, _):
        acc[dy] = dot_chunk(chunk(0, dy))
        return 0

    lax.fori_loop(0, 2, own, 0)

    def with_sides(dy, k, r):
        total = acc[dy, r, :]
        for way in range(2):
            arrived(rx.at[way, dy, r, :], rs_recv.at[way, dy, k])
            total += rx[way, dy, r, :].astype(F32)
        return total

    for k in range(8):
        r = rows((z + FAR[k]) % 8 * 64, 64)
        qy[r, :] = with_sides(1, k, r).astype(BF)
        remote(qy.at[r, :], ry.at[r, :], ry_send.at[k], ry_recv.at[k], dev(0, 1, 0)).start()
    for i in range(EARLY, 4):
        tokens_across(i)
    for k in range(8):
        r = rows((z + FAR[k]) % 8 * 64, 64)
        total = with_sides(0, k, r)
        arrived(ry.at[r, :], ry_recv.at[k])
        total += ry[r, :].astype(F32)
        if k < 7:
            qz[r, :] = total.astype(BF)
            remote(qz.at[r, :], rz.at[k], rz_send.at[k], rz_recv.at[k], dev(0, 0, FAR[k])).start()
        else:
            acc[0, 0:64, :] = total

    for dy in range(2):
        total = part[rows(chunk(2, dy) + z * 64, 64), :].astype(F32)
        for k in range(7):
            arrived(rf.at[dy, k], rf_recv.at[dy, k])
            total += rf[dy, k].astype(F32)
        qf[dy] = total.astype(BF)
        remote(qf.at[dy], ro.at[dy], ro_send.at[dy], ro_recv.at[dy], dev(2, dy, 0)).start()

    def head(i):
        arrived(tg_all.at[tile(i), own_lanes], tg_recv.at[4 + i])
        head_out[tile(i), :] = lax.dot_general(
            tg_all[tile(i), :], hx_all[...], (((1,), (1,)), ((), ())), preferred_element_type=F32
        ).astype(BF)

    def head_step(i, _):
        src = tg_all.at[tile(i), rows((other + core) * T, T)]
        arrived(src, tg_recv.at[i])
        remote(src, src, tg_send.at[4 + i], tg_recv.at[4 + i], twin).start()

        @pl.when(i > 0)
        def _():
            head(i - 1)

        return 0

    arrived(hx_all.at[:, own_lanes], hx_recv.at[2, 0])
    for c2 in range(2):
        for dy in range(2):
            arrived(hx_all.at[0:512, own_lanes], hx_recv.at[c2, dy])
    arrived(tg_all.at[:, own_lanes], tg_recv.at[8])
    lax.fori_loop(0, 4, head_step, 0)
    head(3)

    total = acc[0, 0:64, :]
    for k in range(7):
        arrived(rz.at[k], rz_recv.at[k])
        total += rz[k].astype(F32)
    for dy in range(2):
        arrived(ro.at[dy], ro_recv.at[dy])
        total += ro[dy].astype(F32)
    hg_out[...] = total.astype(BF)

    one = h.at[0:64, :]
    for k in range(8):
        for f in range(2):
            if k or not f:
                sent(one, ag_send_z.at[f, k])
            sent(one, ag_send_y.at[f, k])
            sent(one, ag_send_x.at[0, f, k])
            sent(one, ag_send_x.at[1, f, k])
            sent(one, rs_send.at[0, f, k])
            sent(one, rs_send.at[1, f, k])
            if k < 7:
                sent(one, rf_send.at[f, k])
        sent(one, ry_send.at[k])
        if k < 7:
            sent(one, rz_send.at[k])
    for i in range(2):
        for dy in range(2):
            sent(h.at[0:512, :], hx_send.at[i, dy])
        sent(one, ro_send.at[i])
        for j in range(7):
            sent(st.at[i], st_send.at[i, j])
    sent(h.at[0:1024, :], hx_send.at[2, 0])
    for i in range(8):
        sent(tg.at[0:304, :], tg_send.at[i])
    sent(tg, tg_send.at[8])


def per_device(hidden, head_weight, teacher_codes, teacher_scales, loss_cotangent):
    dma = pltpu.SemaphoreType.DMA
    vmem = pl.BlockSpec(memory_space=pltpu.VMEM)
    hbm = pl.BlockSpec(memory_space=pltpu.HBM)
    hidden_grad, head_grad = pl.pallas_call(
        kernel,
        name="head_backward",
        out_shape=(
            jax.ShapeDtypeStruct((64, T), BF),
            jax.ShapeDtypeStruct((V, 1024), BF),
        ),
        in_specs=[hbm] * 5,
        out_specs=(vmem, vmem),
        scratch_shapes=[
            pltpu.VMEM((38, T), jnp.int32),
            pltpu.VMEM((1, T), F32),
            pltpu.VMEM((4096, T), BF),
            pltpu.VMEM((V, 4096), BF),
            pltpu.VMEM((V, T), jnp.int32),
            pltpu.VMEM((V, T), F32),
            pltpu.VMEM((V, T), F32),
            pltpu.VMEM((V, T), BF),
            pltpu.VMEM((V, 4 * T), BF),
            pltpu.VMEM((1024, 4 * T), BF),
            pltpu.VMEM((4096, T), BF),
            pltpu.VMEM((2, 2, 512, T), BF),
            pltpu.VMEM((2, 7, 64, T), BF),
            pltpu.VMEM((2, 64, T), BF),
            pltpu.VMEM((2, 64, T), BF),
            pltpu.VMEM((2, 512, T), F32),
            pltpu.VMEM((512, T), BF),
            pltpu.VMEM((512, T), BF),
            pltpu.VMEM((512, T), BF),
            pltpu.VMEM((7, 64, T), BF),
            pltpu.VMEM((2, 8, 128), F32),
            pltpu.VMEM((7, 8, 128), F32),
            pltpu.VMEM((7, 8, 128), F32),
            dma((6,)),
            dma((2, 8)),
            dma((2, 8)),
            dma((2, 2, 8)),
            dma((4, 2, 8)),
            dma((3, 2)),
            dma((3, 2)),
            dma((9,)),
            dma((9,)),
            dma((2, 7)),
            dma((2, 7)),
            dma((2, 2, 8)),
            dma((2, 2, 8)),
            dma((2, 7)),
            dma((2, 7)),
            dma((2,)),
            dma((2,)),
            dma((8,)),
            dma((8,)),
            dma((7,)),
            dma((7,)),
        ],
        compiler_params=pltpu.CompilerParams(
            collective_id=0, has_side_effects=True, vmem_limit_bytes=48 << 20
        ),
        cost_estimate=pl.CostEstimate(
            flops=6 * V * T * 4096, bytes_accessed=14 << 20, transcendentals=2 * V * T
        ),
    )(*(
        pltpu.with_memory_space_constraint(a, pltpu.HBM)
        for a in (hidden.T, teacher_scales.T, loss_cotangent.reshape(1, T), head_weight, teacher_codes.T)
    ))
    return hidden_grad.T, head_grad


def solution(mesh):
    return jax.shard_map(
        per_device,
        mesh=mesh,
        in_specs=(P("dp", "vocab"), P("vocab", None), P("dp", "vocab"), P("dp", "vocab"), P("dp")),
        out_specs=(P("dp", "vocab"), P("vocab", "dp")),
        check_vma=False,
    )
```

```python
import jax
import jax.numpy as jnp
from jax import lax
from jax.experimental import pallas as pl
from jax.experimental.pallas import tpu as pltpu
from jax.sharding import PartitionSpec as P

BF = jnp.bfloat16
F32 = jnp.float32
MESH = pl.DeviceIdType.MESH

V = 1216
T = 256
NEAR = (0, 1, 7, 2, 6, 3, 5, 4)
FAR = (4, 3, 5, 2, 6, 1, 7, 0)


def rows(start, size):
    return pl.ds(pl.multiple_of(start, size), size)


def kernel(
    hid_hbm,
    scales_hbm,
    cot_hbm,
    w_hbm,
    codes_hbm,
    hg_out,
    head_out,
    scales,
    cot,
    h,
    w,
    codes,
    teach,
    logits,
    tg,
    tg_all,
    hx_all,
    part,
    rx,
    rz,
    qz,
    qo,
    ro,
    acc,
    st,
    st_z,
    st_xy,
    local_sem,
    ag_send_z,
    ag_send_y,
    ag_send_x,
    ag_recv,
    hx_send,
    hx_recv,
    tg_send,
    tg_recv,
    st_send,
    st_recv,
    rs_send,
    rs_recv,
    rz_send,
    rz_recv,
    ro_send,
    ro_recv,
):
    v = lax.axis_index("vocab")
    d = lax.axis_index("dp")
    x, y, z = v // 16, (v // 8) % 2, v % 8
    yh, core = d // 2, d % 2
    turn = 1 - 2 * core

    def at(dx, dy, dz):
        return ((x + dx) % 4 * 2 + (y + dy) % 2) * 8 + (z + dz) % 8

    def dev(dx, dy, dz):
        return (at(dx, dy, dz), d)

    other = (1 - yh) * 2
    cross = [(at(0, 1, 0), other), (at(0, 1, 0), other + 1)]
    twin = (v, yh * 2 + 1 - core)
    opposite = (v, other + core)

    def remote(src, dst, ss, rs, to):
        return pltpu.make_async_remote_copy(
            src_ref=src, dst_ref=dst, send_sem=ss, recv_sem=rs, device_id=to, device_id_type=MESH
        )

    def arrived(ref, rs):
        remote(ref, ref, local_sem.at[0], rs, twin).wait_recv()

    def sent(ref, ss):
        remote(ref, ref, ss, local_sem.at[0], twin).wait_send()

    barrier = pltpu.get_barrier_semaphore()
    partners = [dev(0, 0, dz) for dz in range(1, 8)]
    partners += [dev(dx, dy, 0) for dx in range(4) for dy in range(2) if dx or dy]
    partners += cross + [twin, opposite]
    for p in partners:
        pl.semaphore_signal(barrier, inc=1, device_id=p, device_id_type=MESH)

    loads = [
        pltpu.make_async_copy(src, dst, local_sem.at[1 + i])
        for i, (src, dst) in enumerate(
            (
                (hid_hbm, h.at[rows(v * 64, 64), :]),
                (scales_hbm, scales),
                (codes_hbm, codes),
                (cot_hbm, cot),
                (w_hbm, w),
            )
        )
    ]
    for load in loads:
        load.start()

    loads[1].wait()
    loads[2].wait()

    def decode(b, total):
        r = rows(b * 32, 32)
        c = codes[r, :]
        field = c >> 3
        mantissa = (c & 7).astype(F32)
        s = scales[pl.ds(b, 1), :]
        digits = jnp.where(field == 0, 2.0 * mantissa, 8.0 + mantissa)
        value = digits * jnp.exp2((field - 10 + s).astype(F32))
        teach[r, :] = value
        return total + value

    total = lax.fori_loop(0, V // 32, decode, jnp.zeros((32, T), F32))
    teacher_sum = jnp.sum(total, axis=0, keepdims=True)

    loads[0].wait()
    loads[3].wait()
    pl.semaphore_wait(barrier, len(partners))

    def block(dx, dy, k):
        return h.at[rows(at(dx, dy, -NEAR[k]) * 64, 64), :]

    def pass_on(b, ss, rs, to):
        remote(b, b, ss, rs, to).start()

    def spread_x(dy, k):
        for i, dx in ((0, 1), (1, -1)):
            pass_on(block(0, dy, k), ag_send_x.at[i, dy, k], ag_recv.at[2 + i, dy, k], dev(dx, 0, 0))

    def spread_y(far, k):
        pass_on(block(2 * far, 0, k), ag_send_y.at[far, k], ag_recv.at[far, 1, k], dev(0, 1, 0))

    def spread_z(far):
        for k in (3, 4, 1, 2):
            pass_on(block(2 * far, 0, 0), ag_send_z.at[far, k], ag_recv.at[far, 0, k], dev(0, 0, NEAR[k]))

    def forward_z(far):
        for k, dz in ((3, 1), (4, -1)):
            pass_on(block(2 * far, 0, k), ag_send_z.at[far, k + 2], ag_recv.at[far, 0, k + 2], dev(0, 0, dz))
        b = h.at[rows(at(2 * far, 0, -2 * turn) * 64, 64), :]
        pass_on(b, ag_send_z.at[far, 7], ag_recv.at[far, 0, 7], dev(0, 0, 2 * turn))

    def chunk(dx, dy):
        return ((x + dx) % 4 * 2 + (y + dy) % 2) * 512

    own_lanes = rows(d * T, T)

    def hidden_across(dx, dy):
        quarter = (x + dx) % 4

        @pl.when(quarter // 2 == 1 - yh)
        def _():
            c2 = quarter % 2
            src = h.at[rows(chunk(dx, dy), 512), :]
            dst = hx_all.at[rows((y + dy) % 2 * 512, 512), own_lanes]
            to = (at(0, 1, 0), other + c2)
            remote(src, dst, hx_send.at[c2, dy], hx_recv.at[core, dy], to).start()

    pass_on(block(0, 0, 0), ag_send_z.at[0, 0], ag_recv.at[1, 0, 0], dev(2, 0, 0))
    spread_z(0)
    spread_x(0, 0)
    spread_y(0, 0)
    def from_z(k):
        arrived(block(0, 0, k), ag_recv.at[0, 0, k])
        if k == 4:
            forward_z(0)
        spread_x(0, k)
        spread_y(0, k)

    def from_y(k):
        arrived(block(0, 1, k), ag_recv.at[0, 1, k])
        spread_x(1, k)

    def from_far(k):
        arrived(block(2, 0, k), ag_recv.at[1, 0, k])
        if k == 0:
            spread_z(1)
        if k == 4:
            forward_z(1)
        spread_y(1, k)

    for step, ks in (
        (from_z, (1, 2)),
        (from_y, (0,)),
        (from_z, (3, 4)),
        (from_far, (0,)),
        (from_y, (1, 2)),
        (from_z, (5, 6)),
        (from_y, (3, 4)),
        (from_z, (7,)),
        (from_far, (3, 4)),
        (from_y, (5, 6)),
        (from_far, (1, 2)),
        (from_y, (7,)),
        (from_far, (5, 6, 7)),
    ):
        for k in ks:
            step(k)
        if step is from_z and 7 in ks:
            hidden_across(0, 0)
        if step is from_y and 7 in ks:
            hidden_across(0, 1)
    hidden_across(2, 0)

    def add_logits(start):
        f = rows(start, 512)
        logits[...] += jnp.dot(w[:, f], h[f, :], preferred_element_type=F32)

    logits[...] = jnp.zeros_like(logits)
    loads[4].wait()

    def dots_near(i, _):
        add_logits(chunk(0, i))
        return 0

    lax.fori_loop(0, 2, dots_near, 0)
    add_logits(chunk(2, 0))
    for dy in range(2):
        for k in range(8):
            for i, dx in ((0, 1), (1, -1)):
                arrived(block(-dx, dy, k), ag_recv.at[2 + i, dy, k])
        hidden_across(1, dy)
        hidden_across(3, dy)
        if dy == 0:

            def dots_side(i, _):
                add_logits(chunk(1 + 2 * i, 0))
                return 0

            lax.fori_loop(0, 2, dots_side, 0)
    for k in range(8):
        arrived(block(2, 1, k), ag_recv.at[1, 1, k])
    hidden_across(2, 1)
    src = h.at[rows((yh * 2 + 1 - core) * 1024, 1024), :]
    remote(src, hx_all.at[:, own_lanes], hx_send.at[2, 0], hx_recv.at[2, 0], twin).start()
    hx_all[:, own_lanes] = h[rows(d * 1024, 1024), :]

    def dots_last(i, _):
        add_logits(chunk(1 + i, 1))
        return 0

    lax.fori_loop(0, 3, dots_last, 0)

    def top(b, m):
        return jnp.maximum(m, logits[rows(b * 32, 32), :])

    m = lax.fori_loop(1, V // 32, top, logits[0:32, :])
    local_max = jnp.max(m, axis=0, keepdims=True)

    def exps(b, s):
        r = rows(b * 32, 32)
        e = jnp.exp(logits[r, :] - local_max)
        logits[r, :] = e
        return s + e

    s = lax.fori_loop(0, V // 32, exps, jnp.zeros((32, T), F32))
    local_sum = jnp.sum(s, axis=0, keepdims=True)

    def share(m, s, t, stage, buf, peers):
        for n, value in enumerate((m, s, t)):
            for half in range(2):
                st[stage, 2 * n + half : 2 * n + half + 1, :] = value[:, half * 128 : half * 128 + 128]
        for j, p in enumerate(peers):
            remote(st.at[stage], buf.at[j], st_send.at[stage, j], st_recv.at[stage, j], p).start()
        for j in range(7):
            arrived(buf.at[j], st_recv.at[stage, j])
        m, s, t = (st[stage, 2 * n : 2 * n + 2, :] for n in range(3))
        best = m
        for j in range(7):
            best = jnp.maximum(best, buf[j, 0:2, :])
        s = s * jnp.exp(m - best)
        for j in range(7):
            s += buf[j, 2:4, :] * jnp.exp(buf[j, 0:2, :] - best)
            t += buf[j, 4:6, :]
        return tuple(jnp.concatenate([a[0:1, :], a[1:2, :]], axis=1) for a in (best, s, t))

    st[...] = jnp.zeros_like(st)
    along_z = [dev(0, 0, dz) for dz in FAR[:7]]
    along_xy = [dev(dx, dy, 0) for dx, dy in ((2, 1), (2, 0), (1, 1), (3, 1), (1, 0), (3, 0), (0, 1))]
    row_max, row_sum, row_teach = share(local_max, local_sum, teacher_sum, 0, st_z, along_z)
    row_max, row_sum, row_teach = share(row_max, row_sum, row_teach, 1, st_xy, along_xy)

    up = cot[...] * jnp.exp(local_max - row_max) / row_sum
    down = cot[...] / row_teach

    def tile(i):
        return rows(i * 304, 304)

    def tokens_across(i):
        dst = tg_all.at[tile(i), own_lanes]
        remote(tg.at[tile(i), :], dst, tg_send.at[i], tg_recv.at[i], opposite).start()

    def grads(b, _):
        r = rows(b * 32, 32)
        g = (logits[r, :] * up - teach[r, :] * down).astype(BF)
        tg[r, :] = g
        tg_all[r, own_lanes] = g
        return 0

    for i, (lo, hi) in enumerate(((0, 10), (10, 19), (19, 29), (29, 38))):
        lax.fori_loop(lo, hi, grads, 0)
        tokens_across(i)
    remote(tg, tg_all.at[:, own_lanes], tg_send.at[8], tg_recv.at[8], twin).start()

    def dot_chunk(start):
        return lax.dot_general(
            w[:, rows(start, 512)], tg[...], (((0,), (0,)), ((), ())), preferred_element_type=F32
        )

    def along_z(plane, dy, slot, src, dz):
        ss, rs = rz_send.at[plane, dy, slot], rz_recv.at[plane, dy, slot]
        remote(src, rz.at[plane, dy, slot], ss, rs, dev(0, 0, dz)).start()

    def came(plane, dy, slot):
        arrived(rz.at[plane, dy, slot], rz_recv.at[plane, dy, slot])
        return rz[plane, dy, slot].astype(F32)

    def two_away(plane, dy, mine):
        for i in range(2):
            a = (core + i) % 2
            dz = 2 - 4 * a
            total = mine(dz) + came(plane, dy, 1 + a)
            if i == 0:
                total += came(plane, dy, 0)
            qz[plane, dy, 3 + i] = total.astype(BF)
            along_z(plane, dy, 3 + a, qz.at[plane, dy, 3 + i], dz)

    def over_z(plane, dy, mine):
        total = mine(0)
        for slot in range(3, 7):
            total += came(plane, dy, slot)
        return total

    straight = ((4, 0, 2 * turn), (3, 1, 1), (-3, 2, -1), (1, 5, 1), (-1, 6, -1))

    def side(way, dy):
        start = chunk(1 + 2 * way, dy)
        part[rows(start, 512), :] = dot_chunk(start).astype(BF)
        for k in range(8):
            zz = (z + FAR[k]) % 8
            src = part.at[rows(start + zz * 64, 64), :]
            dst = rx.at[way, dy, rows(zz * 64, 64), :]
            remote(src, dst, rs_send.at[way, dy, k], rs_recv.at[way, dy, k], dev(1 - 2 * way, 0, 0)).start()

    def far(dy):
        start = chunk(2, dy)
        part[rows(start, 512), :] = dot_chunk(start).astype(BF)
        for dz, slot, to in straight:
            along_z(0, dy, slot, part.at[rows(start + (z + dz) % 8 * 64, 64), :], to)

    def dots(i, _):
        @pl.when((i == 0) | (i == 3))
        def _():
            far(1 - i // 3)

        @pl.when((i == 1) | (i == 2))
        def _():
            side(i - 1, 1)

        @pl.when((i == 4) | (i == 5))
        def _():
            side(i - 4, 0)

        @pl.when(i > 5)
        def _():
            acc[7 - i] = dot_chunk(chunk(0, 7 - i))

        return 0

    lax.fori_loop(0, 8, dots, 0)

    def far_block(dy):
        return lambda dz: part[rows(chunk(2, dy) + (z + dz) % 8 * 64, 64), :].astype(F32)

    def near_block(dy):
        return lambda dz: acc[dy, rows((z + dz) % 8 * 64, 64), :]

    def with_sides(dy, k):
        r = rows((z + FAR[k]) % 8 * 64, 64)
        total = acc[dy, r, :]
        for way in range(2):
            arrived(rx.at[way, dy, r, :], rs_recv.at[way, dy, k])
            total += rx[way, dy, r, :].astype(F32)
        return r, total

    def near(dy, ks):
        for k in ks:
            r, total = with_sides(dy, k)
            acc[dy, r, :] = total
            for dz, slot, to in straight:
                if dz % 8 == FAR[k]:
                    qz[1, dy, slot] = total.astype(BF)
                    along_z(1, dy, slot, qz.at[1, dy, slot], to)

    def give(i, total, to):
        qo[i] = total.astype(BF)
        remote(qo.at[i], ro.at[i], ro_send.at[i], ro_recv.at[i], to).start()

    def to_twin(i):
        src = tg_all.at[tile(i), rows((other + core) * T, T)]
        arrived(src, tg_recv.at[i])
        remote(src, src, tg_send.at[4 + i], tg_recv.at[4 + i], twin).start()

    def hidden_here():
        arrived(hx_all.at[:, own_lanes], hx_recv.at[2, 0])
        for c2 in range(2):
            for dy in range(2):
                arrived(hx_all.at[0:512, own_lanes], hx_recv.at[c2, dy])
        arrived(tg_all.at[:, own_lanes], tg_recv.at[8])

    def head(i):
        arrived(tg_all.at[tile(i), own_lanes], tg_recv.at[4 + i])
        head_out[tile(i), :] = lax.dot_general(
            tg_all[tile(i), :], hx_all[...], (((1,), (1,)), ((), ())), preferred_element_type=F32
        ).astype(BF)

    two_away(0, 1, far_block(1))
    near(1, (0, 1, 2))
    two_away(0, 0, far_block(0))
    near(1, (3, 4, 5, 6))
    two_away(1, 1, near_block(1))
    near(1, (7,))
    for dy in (1, 0):
        give(dy, over_z(0, dy, far_block(dy)), dev(2, dy, 0))
    near(0, (0, 1, 2, 3))
    give(2, over_z(1, 1, near_block(1)), dev(0, 1, 0))
    near(0, (4, 5))
    to_twin(0)
    two_away(1, 0, near_block(0))
    to_twin(1)
    hidden_here()
    head(0)
    near(0, (6, 7))
    to_twin(2)
    head(1)
    to_twin(3)
    head(2)
    head(3)

    total = over_z(1, 0, near_block(0))
    for i in range(3):
        arrived(ro.at[i], ro_recv.at[i])
        total += ro[i].astype(F32)
    hg_out[...] = total.astype(BF)

    one = h.at[0:64, :]
    for k in range(8):
        for f in range(2):
            if k or not f:
                sent(one, ag_send_z.at[f, k])
            sent(one, ag_send_y.at[f, k])
            sent(one, ag_send_x.at[0, f, k])
            sent(one, ag_send_x.at[1, f, k])
            sent(one, rs_send.at[0, f, k])
            sent(one, rs_send.at[1, f, k])
            if k < 7:
                for dy in range(2):
                    sent(one, rz_send.at[f, dy, k])
    for i in range(3):
        sent(one, ro_send.at[i])
    for i in range(2):
        for dy in range(2):
            sent(h.at[0:512, :], hx_send.at[i, dy])
        for j in range(7):
            sent(st.at[i], st_send.at[i, j])
    sent(h.at[0:1024, :], hx_send.at[2, 0])
    for i in range(8):
        sent(tg.at[0:304, :], tg_send.at[i])
    sent(tg, tg_send.at[8])


def per_device(hidden, head_weight, teacher_codes, teacher_scales, loss_cotangent):
    dma = pltpu.SemaphoreType.DMA
    vmem = pl.BlockSpec(memory_space=pltpu.VMEM)
    hbm = pl.BlockSpec(memory_space=pltpu.HBM)
    hidden_grad, head_grad = pl.pallas_call(
        kernel,
        name="head_backward",
        out_shape=(
            jax.ShapeDtypeStruct((64, T), BF),
            jax.ShapeDtypeStruct((V, 1024), BF),
        ),
        in_specs=[hbm] * 5,
        out_specs=(vmem, vmem),
        scratch_shapes=[
            pltpu.VMEM((38, T), jnp.int32),
            pltpu.VMEM((1, T), F32),
            pltpu.VMEM((4096, T), BF),
            pltpu.VMEM((V, 4096), BF),
            pltpu.VMEM((V, T), jnp.int32),
            pltpu.VMEM((V, T), F32),
            pltpu.VMEM((V, T), F32),
            pltpu.VMEM((V, T), BF),
            pltpu.VMEM((V, 4 * T), BF),
            pltpu.VMEM((1024, 4 * T), BF),
            pltpu.VMEM((4096, T), BF),
            pltpu.VMEM((2, 2, 512, T), BF),
            pltpu.VMEM((2, 2, 7, 64, T), BF),
            pltpu.VMEM((2, 2, 7, 64, T), BF),
            pltpu.VMEM((3, 64, T), BF),
            pltpu.VMEM((3, 64, T), BF),
            pltpu.VMEM((2, 512, T), F32),
            pltpu.VMEM((2, 8, 128), F32),
            pltpu.VMEM((7, 8, 128), F32),
            pltpu.VMEM((7, 8, 128), F32),
            dma((6,)),
            dma((2, 8)),
            dma((2, 8)),
            dma((2, 2, 8)),
            dma((4, 2, 8)),
            dma((3, 2)),
            dma((3, 2)),
            dma((9,)),
            dma((9,)),
            dma((2, 7)),
            dma((2, 7)),
            dma((2, 2, 8)),
            dma((2, 2, 8)),
            dma((2, 2, 7)),
            dma((2, 2, 7)),
            dma((3,)),
            dma((3,)),
        ],
        compiler_params=pltpu.CompilerParams(
            collective_id=0, has_side_effects=True, vmem_limit_bytes=48 << 20
        ),
        cost_estimate=pl.CostEstimate(
            flops=6 * V * T * 4096, bytes_accessed=14 << 20, transcendentals=2 * V * T
        ),
    )(*(
        pltpu.with_memory_space_constraint(a, pltpu.HBM)
        for a in (hidden.T, teacher_scales.T, loss_cotangent.reshape(1, T), head_weight, teacher_codes.T)
    ))
    return hidden_grad.T, head_grad


def solution(mesh):
    return jax.shard_map(
        per_device,
        mesh=mesh,
        in_specs=(P("dp", "vocab"), P("vocab", None), P("dp", "vocab"), P("dp", "vocab"), P("dp")),
        out_specs=(P("dp", "vocab"), P("vocab", "dp")),
        check_vma=False,
    )
```

```python
import jax
import jax.numpy as jnp
from jax import lax
from jax.experimental import pallas as pl
from jax.experimental.pallas import tpu as pltpu
from jax.sharding import PartitionSpec as P

BF = jnp.bfloat16
F32 = jnp.float32
MESH = pl.DeviceIdType.MESH

V = 1216
T = 256
NEAR = (0, 1, 7, 2, 6, 3, 5, 4)
FAR = (4, 3, 5, 2, 6, 1, 7, 0)


def rows(start, size):
    return pl.ds(pl.multiple_of(start, size), size)


def kernel(
    hid_hbm,
    scales_hbm,
    cot_hbm,
    w_hbm,
    codes_hbm,
    hg_out,
    head_out,
    scales,
    cot,
    h,
    w,
    codes,
    teach,
    logits,
    tg,
    tg_all,
    hx_all,
    part,
    rx,
    rz,
    qz,
    qo,
    ro,
    acc,
    st,
    st_z,
    st_xy,
    local_sem,
    ag_send_z,
    ag_send_y,
    ag_send_x,
    ag_recv,
    hx_send,
    hx_recv,
    tg_send,
    tg_recv,
    st_send,
    st_recv,
    rs_send,
    rs_recv,
    rz_send,
    rz_recv,
    ro_send,
    ro_recv,
):
    v = lax.axis_index("vocab")
    d = lax.axis_index("dp")
    x, y, z = v // 16, (v // 8) % 2, v % 8
    yh, core = d // 2, d % 2
    turn = 1 - 2 * core

    def at(dx, dy, dz):
        return ((x + dx) % 4 * 2 + (y + dy) % 2) * 8 + (z + dz) % 8

    def dev(dx, dy, dz):
        return (at(dx, dy, dz), d)

    other = (1 - yh) * 2
    cross = [(at(0, 1, 0), other), (at(0, 1, 0), other + 1)]
    twin = (v, yh * 2 + 1 - core)
    opposite = (v, other + core)

    def remote(src, dst, ss, rs, to):
        return pltpu.make_async_remote_copy(
            src_ref=src, dst_ref=dst, send_sem=ss, recv_sem=rs, device_id=to, device_id_type=MESH
        )

    def arrived(ref, rs):
        remote(ref, ref, local_sem.at[0], rs, twin).wait_recv()

    def sent(ref, ss):
        remote(ref, ref, ss, local_sem.at[0], twin).wait_send()

    barrier = pltpu.get_barrier_semaphore()
    partners = [dev(0, 0, dz) for dz in range(1, 8)]
    partners += [dev(dx, dy, 0) for dx in range(4) for dy in range(2) if dx or dy]
    partners += cross + [twin, opposite]
    for p in partners:
        pl.semaphore_signal(barrier, inc=1, device_id=p, device_id_type=MESH)

    loads = [
        pltpu.make_async_copy(src, dst, local_sem.at[1 + i])
        for i, (src, dst) in enumerate(
            (
                (hid_hbm, h.at[rows(v * 64, 64), :]),
                (scales_hbm, scales),
                (codes_hbm, codes),
                (cot_hbm, cot),
                (w_hbm, w),
            )
        )
    ]
    for load in loads:
        load.start()

    loads[1].wait()
    loads[2].wait()

    def decode(b, total):
        r = rows(b * 32, 32)
        c = codes[r, :]
        field = c >> 3
        mantissa = (c & 7).astype(F32)
        s = scales[pl.ds(b, 1), :]
        digits = jnp.where(field == 0, 2.0 * mantissa, 8.0 + mantissa)
        value = digits * jnp.exp2((field - 10 + s).astype(F32))
        teach[r, :] = value
        return total + value

    total = lax.fori_loop(0, V // 32, decode, jnp.zeros((32, T), F32))
    teacher_sum = jnp.sum(total, axis=0, keepdims=True)

    loads[0].wait()
    loads[3].wait()
    pl.semaphore_wait(barrier, len(partners))

    def block(dx, dy, k):
        return h.at[rows(at(dx, dy, -NEAR[k]) * 64, 64), :]

    def pass_on(b, ss, rs, to):
        remote(b, b, ss, rs, to).start()

    def spread_x(dy, k):
        for i, dx in ((0, 1), (1, -1)):
            pass_on(block(0, dy, k), ag_send_x.at[i, dy, k], ag_recv.at[2 + i, dy, k], dev(dx, 0, 0))

    def spread_y(far, k):
        pass_on(block(2 * far, 0, k), ag_send_y.at[far, k], ag_recv.at[far, 1, k], dev(0, 1, 0))

    def spread_z(far):
        for k in (3, 4, 1, 2):
            pass_on(block(2 * far, 0, 0), ag_send_z.at[far, k], ag_recv.at[far, 0, k], dev(0, 0, NEAR[k]))

    def forward_z(far):
        for k, dz in ((3, 1), (4, -1)):
            pass_on(block(2 * far, 0, k), ag_send_z.at[far, k + 2], ag_recv.at[far, 0, k + 2], dev(0, 0, dz))
        b = h.at[rows(at(2 * far, 0, -2 * turn) * 64, 64), :]
        pass_on(b, ag_send_z.at[far, 7], ag_recv.at[far, 0, 7], dev(0, 0, 2 * turn))

    def chunk(dx, dy):
        return ((x + dx) % 4 * 2 + (y + dy) % 2) * 512

    own_lanes = rows(d * T, T)

    def hidden_across(dx, dy):
        quarter = (x + dx) % 4

        @pl.when(quarter // 2 == 1 - yh)
        def _():
            c2 = quarter % 2
            src = h.at[rows(chunk(dx, dy), 512), :]
            dst = hx_all.at[rows((y + dy) % 2 * 512, 512), own_lanes]
            to = (at(0, 1, 0), other + c2)
            remote(src, dst, hx_send.at[c2, dy], hx_recv.at[core, dy], to).start()

    pass_on(block(0, 0, 0), ag_send_z.at[0, 0], ag_recv.at[1, 0, 0], dev(2, 0, 0))
    spread_z(0)
    spread_x(0, 0)
    spread_y(0, 0)
    def from_z(k):
        arrived(block(0, 0, k), ag_recv.at[0, 0, k])
        if k == 4:
            forward_z(0)
        spread_x(0, k)
        spread_y(0, k)

    def from_y(k):
        arrived(block(0, 1, k), ag_recv.at[0, 1, k])
        spread_x(1, k)

    def from_far(k):
        arrived(block(2, 0, k), ag_recv.at[1, 0, k])
        if k == 0:
            spread_z(1)
        if k == 4:
            forward_z(1)
        spread_y(1, k)

    for step, ks in (
        (from_z, (1, 2)),
        (from_y, (0,)),
        (from_z, (3, 4)),
        (from_far, (0,)),
        (from_y, (1, 2)),
        (from_z, (5, 6)),
        (from_y, (3, 4)),
        (from_z, (7,)),
        (from_far, (3, 4)),
        (from_y, (5, 6)),
        (from_far, (1, 2)),
        (from_y, (7,)),
        (from_far, (5, 6, 7)),
    ):
        for k in ks:
            step(k)
        if step is from_z and 7 in ks:
            hidden_across(0, 0)
        if step is from_y and 7 in ks:
            hidden_across(0, 1)
    hidden_across(2, 0)

    def add_logits(start):
        f = rows(start, 512)
        logits[...] += jnp.dot(w[:, f], h[f, :], preferred_element_type=F32)

    logits[...] = jnp.zeros_like(logits)
    loads[4].wait()

    def dots_near(i, _):
        add_logits(chunk(0, i))
        return 0

    lax.fori_loop(0, 2, dots_near, 0)
    add_logits(chunk(2, 0))
    for dy in range(2):
        for k in range(8):
            for i, dx in ((0, 1), (1, -1)):
                arrived(block(-dx, dy, k), ag_recv.at[2 + i, dy, k])
        hidden_across(1, dy)
        hidden_across(3, dy)
        if dy == 0:

            def dots_side(i, _):
                add_logits(chunk(1 + 2 * i, 0))
                return 0

            lax.fori_loop(0, 2, dots_side, 0)
    for k in range(8):
        arrived(block(2, 1, k), ag_recv.at[1, 1, k])
    hidden_across(2, 1)
    src = h.at[rows((yh * 2 + 1 - core) * 1024, 1024), :]
    remote(src, hx_all.at[:, own_lanes], hx_send.at[2, 0], hx_recv.at[2, 0], twin).start()
    hx_all[:, own_lanes] = h[rows(d * 1024, 1024), :]

    def dots_last(i, _):
        add_logits(chunk(1 + i, 1))
        return 0

    lax.fori_loop(0, 3, dots_last, 0)

    def top(b, m):
        return jnp.maximum(m, logits[rows(b * 32, 32), :])

    m = lax.fori_loop(1, V // 32, top, logits[0:32, :])
    local_max = jnp.max(m, axis=0, keepdims=True)

    def exps(b, s):
        r = rows(b * 32, 32)
        e = jnp.exp(logits[r, :] - local_max)
        logits[r, :] = e
        return s + e

    s = lax.fori_loop(0, V // 32, exps, jnp.zeros((32, T), F32))
    local_sum = jnp.sum(s, axis=0, keepdims=True)

    def share(m, s, t, stage, buf, peers):
        for n, value in enumerate((m, s, t)):
            for half in range(2):
                st[stage, 2 * n + half : 2 * n + half + 1, :] = value[:, half * 128 : half * 128 + 128]
        for j, p in enumerate(peers):
            remote(st.at[stage], buf.at[j], st_send.at[stage, j], st_recv.at[stage, j], p).start()
        for j in range(7):
            arrived(buf.at[j], st_recv.at[stage, j])
        m, s, t = (st[stage, 2 * n : 2 * n + 2, :] for n in range(3))
        best = m
        for j in range(7):
            best = jnp.maximum(best, buf[j, 0:2, :])
        s = s * jnp.exp(m - best)
        for j in range(7):
            s += buf[j, 2:4, :] * jnp.exp(buf[j, 0:2, :] - best)
            t += buf[j, 4:6, :]
        return tuple(jnp.concatenate([a[0:1, :], a[1:2, :]], axis=1) for a in (best, s, t))

    st[...] = jnp.zeros_like(st)
    along_z = [dev(0, 0, dz) for dz in FAR[:7]]
    along_xy = [dev(dx, dy, 0) for dx, dy in ((2, 1), (2, 0), (1, 1), (3, 1), (1, 0), (3, 0), (0, 1))]
    row_max, row_sum, row_teach = share(local_max, local_sum, teacher_sum, 0, st_z, along_z)
    row_max, row_sum, row_teach = share(row_max, row_sum, row_teach, 1, st_xy, along_xy)

    up = cot[...] * jnp.exp(local_max - row_max) / row_sum
    down = cot[...] / row_teach

    def tile(i):
        return rows(i * 304, 304)

    def tokens_across(i):
        dst = tg_all.at[tile(i), own_lanes]
        remote(tg.at[tile(i), :], dst, tg_send.at[i], tg_recv.at[i], opposite).start()

    def grads(b, _):
        r = rows(b * 32, 32)
        g = (logits[r, :] * up - teach[r, :] * down).astype(BF)
        tg[r, :] = g
        tg_all[r, own_lanes] = g
        return 0

    for i, (lo, hi) in enumerate(((0, 10), (10, 19), (19, 29), (29, 38))):
        lax.fori_loop(lo, hi, grads, 0)
        tokens_across(i)
    remote(tg, tg_all.at[:, own_lanes], tg_send.at[8], tg_recv.at[8], twin).start()

    def dot_chunk(start):
        return lax.dot_general(
            w[:, rows(start, 512)], tg[...], (((0,), (0,)), ((), ())), preferred_element_type=F32
        )

    def along_z(plane, dy, slot, src, dz):
        ss, rs = rz_send.at[plane, dy, slot], rz_recv.at[plane, dy, slot]
        remote(src, rz.at[plane, dy, slot], ss, rs, dev(0, 0, dz)).start()

    def came(plane, dy, slot):
        arrived(rz.at[plane, dy, slot], rz_recv.at[plane, dy, slot])
        return rz[plane, dy, slot].astype(F32)

    def two_away(plane, dy, mine):
        for i in range(2):
            a = (core + i) % 2
            dz = 2 - 4 * a
            total = mine(dz) + came(plane, dy, 1 + a)
            if i == 0:
                total += came(plane, dy, 0)
            qz[plane, dy, 3 + i] = total.astype(BF)
            along_z(plane, dy, 3 + a, qz.at[plane, dy, 3 + i], dz)

    def over_z(plane, dy, mine):
        total = mine(0)
        for slot in range(3, 7):
            total += came(plane, dy, slot)
        return total

    straight = ((4, 0, 2 * turn), (3, 1, 1), (-3, 2, -1), (1, 5, 1), (-1, 6, -1))

    def side(way, dy):
        start = chunk(1 + 2 * way, dy)
        part[rows(start, 512), :] = dot_chunk(start).astype(BF)
        for k in range(8):
            zz = (z + FAR[k]) % 8
            src = part.at[rows(start + zz * 64, 64), :]
            dst = rx.at[way, dy, rows(zz * 64, 64), :]
            remote(src, dst, rs_send.at[way, dy, k], rs_recv.at[way, dy, k], dev(1 - 2 * way, 0, 0)).start()

    def far(dy):
        start = chunk(2, dy)
        part[rows(start, 512), :] = dot_chunk(start).astype(BF)
        for dz, slot, to in straight:
            along_z(0, dy, slot, part.at[rows(start + (z + dz) % 8 * 64, 64), :], to)

    def dots(i, _):
        @pl.when((i == 0) | (i == 3))
        def _():
            far(1 - i // 3)

        @pl.when((i == 1) | (i == 2))
        def _():
            side(i - 1, 1)

        @pl.when((i == 4) | (i == 5))
        def _():
            side(i - 4, 0)

        @pl.when(i > 5)
        def _():
            acc[7 - i] = dot_chunk(chunk(0, 7 - i))

        return 0

    lax.fori_loop(0, 8, dots, 0)

    def far_block(dy):
        return lambda dz: part[rows(chunk(2, dy) + (z + dz) % 8 * 64, 64), :].astype(F32)

    def near_block(dy):
        return lambda dz: acc[dy, rows((z + dz) % 8 * 64, 64), :]

    def with_sides(dy, k):
        r = rows((z + FAR[k]) % 8 * 64, 64)
        total = acc[dy, r, :]
        for way in range(2):
            arrived(rx.at[way, dy, r, :], rs_recv.at[way, dy, k])
            total += rx[way, dy, r, :].astype(F32)
        return r, total

    def near(dy, ks):
        for k in ks:
            r, total = with_sides(dy, k)
            acc[dy, r, :] = total
            for dz, slot, to in straight:
                if dz % 8 == FAR[k]:
                    qz[1, dy, slot] = total.astype(BF)
                    along_z(1, dy, slot, qz.at[1, dy, slot], to)

    def give(i, total, to):
        qo[i] = total.astype(BF)
        remote(qo.at[i], ro.at[i], ro_send.at[i], ro_recv.at[i], to).start()

    def to_twin(i):
        src = tg_all.at[tile(i), rows((other + core) * T, T)]
        arrived(src, tg_recv.at[i])
        remote(src, src, tg_send.at[4 + i], tg_recv.at[4 + i], twin).start()

    def hidden_here():
        arrived(hx_all.at[:, own_lanes], hx_recv.at[2, 0])
        for c2 in range(2):
            for dy in range(2):
                arrived(hx_all.at[0:512, own_lanes], hx_recv.at[c2, dy])
        arrived(tg_all.at[:, own_lanes], tg_recv.at[8])

    def head(i):
        arrived(tg_all.at[tile(i), own_lanes], tg_recv.at[4 + i])
        head_out[tile(i), :] = lax.dot_general(
            tg_all[tile(i), :], hx_all[...], (((1,), (1,)), ((), ())), preferred_element_type=F32
        ).astype(BF)

    two_away(0, 1, far_block(1))
    near(1, (0, 1, 2))
    two_away(0, 0, far_block(0))
    near(1, (3, 4, 5, 6))
    two_away(1, 1, near_block(1))
    near(1, (7,))
    for dy in (1, 0):
        give(dy, over_z(0, dy, far_block(dy)), dev(2, dy, 0))
    near(0, (0, 1, 2, 3))
    give(2, over_z(1, 1, near_block(1)), dev(0, 1, 0))
    near(0, (4, 5))
    to_twin(0)
    two_away(1, 0, near_block(0))
    to_twin(1)
    hidden_here()
    head(0)
    near(0, (6, 7))
    to_twin(2)
    to_twin(3)
    head(1)
    head(2)
    head(3)

    total = over_z(1, 0, near_block(0))
    for i in range(3):
        arrived(ro.at[i], ro_recv.at[i])
        total += ro[i].astype(F32)
    hg_out[...] = total.astype(BF)

    one = h.at[0:64, :]
    for k in range(8):
        for f in range(2):
            if k or not f:
                sent(one, ag_send_z.at[f, k])
            sent(one, ag_send_y.at[f, k])
            sent(one, ag_send_x.at[0, f, k])
            sent(one, ag_send_x.at[1, f, k])
            sent(one, rs_send.at[0, f, k])
            sent(one, rs_send.at[1, f, k])
            if k < 7:
                for dy in range(2):
                    sent(one, rz_send.at[f, dy, k])
    for i in range(3):
        sent(one, ro_send.at[i])
    for i in range(2):
        for dy in range(2):
            sent(h.at[0:512, :], hx_send.at[i, dy])
        for j in range(7):
            sent(st.at[i], st_send.at[i, j])
    sent(h.at[0:1024, :], hx_send.at[2, 0])
    for i in range(8):
        sent(tg.at[0:304, :], tg_send.at[i])
    sent(tg, tg_send.at[8])


def per_device(hidden, head_weight, teacher_codes, teacher_scales, loss_cotangent):
    dma = pltpu.SemaphoreType.DMA
    vmem = pl.BlockSpec(memory_space=pltpu.VMEM)
    hbm = pl.BlockSpec(memory_space=pltpu.HBM)
    hidden_grad, head_grad = pl.pallas_call(
        kernel,
        name="head_backward",
        out_shape=(
            jax.ShapeDtypeStruct((64, T), BF),
            jax.ShapeDtypeStruct((V, 1024), BF),
        ),
        in_specs=[hbm] * 5,
        out_specs=(vmem, vmem),
        scratch_shapes=[
            pltpu.VMEM((38, T), jnp.int32),
            pltpu.VMEM((1, T), F32),
            pltpu.VMEM((4096, T), BF),
            pltpu.VMEM((V, 4096), BF),
            pltpu.VMEM((V, T), jnp.int32),
            pltpu.VMEM((V, T), F32),
            pltpu.VMEM((V, T), F32),
            pltpu.VMEM((V, T), BF),
            pltpu.VMEM((V, 4 * T), BF),
            pltpu.VMEM((1024, 4 * T), BF),
            pltpu.VMEM((4096, T), BF),
            pltpu.VMEM((2, 2, 512, T), BF),
            pltpu.VMEM((2, 2, 7, 64, T), BF),
            pltpu.VMEM((2, 2, 7, 64, T), BF),
            pltpu.VMEM((3, 64, T), BF),
            pltpu.VMEM((3, 64, T), BF),
            pltpu.VMEM((2, 512, T), F32),
            pltpu.VMEM((2, 8, 128), F32),
            pltpu.VMEM((7, 8, 128), F32),
            pltpu.VMEM((7, 8, 128), F32),
            dma((6,)),
            dma((2, 8)),
            dma((2, 8)),
            dma((2, 2, 8)),
            dma((4, 2, 8)),
            dma((3, 2)),
            dma((3, 2)),
            dma((9,)),
            dma((9,)),
            dma((2, 7)),
            dma((2, 7)),
            dma((2, 2, 8)),
            dma((2, 2, 8)),
            dma((2, 2, 7)),
            dma((2, 2, 7)),
            dma((3,)),
            dma((3,)),
        ],
        compiler_params=pltpu.CompilerParams(
            collective_id=0, has_side_effects=True, vmem_limit_bytes=48 << 20
        ),
        cost_estimate=pl.CostEstimate(
            flops=6 * V * T * 4096, bytes_accessed=14 << 20, transcendentals=2 * V * T
        ),
    )(*(
        pltpu.with_memory_space_constraint(a, pltpu.HBM)
        for a in (hidden.T, teacher_scales.T, loss_cotangent.reshape(1, T), head_weight, teacher_codes.T)
    ))
    return hidden_grad.T, head_grad


def solution(mesh):
    return jax.shard_map(
        per_device,
        mesh=mesh,
        in_specs=(P("dp", "vocab"), P("vocab", None), P("dp", "vocab"), P("dp", "vocab"), P("dp")),
        out_specs=(P("dp", "vocab"), P("vocab", "dp")),
        check_vma=False,
    )
```
